128 devices in a mesh: blk: 8 (over x, core), narrow: 16 (over y, z).
Axes of the slice: x: 4, y: 4, z: 4, core: 2. Of those that a mesh axis runs over, the one named last changes fastest.
Arguments:
- node_feats: bfloat16 [262144, 128], P(('blk', 'narrow')), may hold values from -6 to 6
- history: bfloat16 [262144, 1024], P(('blk', 'narrow')), may hold values from -6 to 6
- tile_src: int32 [2048, 2], P(('blk', 'narrow')), may hold values from 0 to 2047, as said below
- tile_count: int32 [2048], P(('blk', 'narrow')), may hold values from 1 to 2
- tile_edges: bfloat16 [2048, 2, 128, 128], P(('blk', 'narrow')), may hold values from 0 to 1, as said below
- w1_self: bfloat16 [128, 1024], replicated, may hold values from -0.5 to 0.5
- w1_nbr: bfloat16 [128, 1024], replicated, may hold values from -0.5 to 0.5
- bias_one: float32 [1024], replicated, may hold values from -3 to 3
- gain_one: float32 [1024], replicated, may hold values from 0.5 to 1.5
- w2_self: bfloat16 [1024, 1024], replicated, may hold values from -0.1875 to 0.1875
- w2_nbr: bfloat16 [1024, 1024], replicated, may hold values from -0.1875 to 0.1875
- bias_two: float32 [1024], replicated, may hold values from -3 to 3
- gain_two: float32 [1024], replicated, may hold values from 0.5 to 1.5
Outputs:
- fresh_history: bfloat16 [262144, 1024], P(('blk', 'narrow'))
- embeddings: bfloat16 [262144, 1024], P(('blk', 'narrow'))
The draws below stay inside these ranges and needn't reach their ends.
Inputs may be any that keep to these rules, and one draw needn't show every extreme that they name: `tile_src`: node block g is stored on device g // 16 of the order blk+narrow (blk slowest), as its block g % 16. For the 16 block rows of one device (r, m), exactly 1 of its tiles name blocks of each device (r, m2) and exactly 1 name blocks of each device ((r + 1) % 8, m2), for all 16 values of m2. `tile_edges`: every entry is 0 or 1; tiles past tile_count are padding and hold arbitrary entries.
All inputs are finite; a program needn't handle non-finite values.
Results may differ from the reference program's by a relative error of at most 0.0045.
Values may be sent and summed in bfloat16 or wider, within the bound.
A program may use at most 128 MiB of HBM per device.

```python
import jax
import jax.numpy as jnp
from jax import lax

BLOCK = 128
FEAT = 128
WIDTH = 1024
TILES = 2
BLK_DEV = 16
BLOCKS = 2048
NODES = 262144
CYCLE = 8
PEERS = 16
PER_PEER = 1


def draw_tile_src(key, part):
    device_count = BLOCKS // BLK_DEV
    tile_total = BLK_DEV * TILES
    device_keys = jax.random.split(jax.random.fold_in(key, 11), device_count)

    def shuffle(one_key):
        return jax.random.permutation(one_key, tile_total).astype(jnp.int32)
    slots = jax.vmap(shuffle)(device_keys)
    route_key = slots // PER_PEER
    peer_pick = route_key // 2
    row_step = route_key % 2
    device_ids = jnp.arange(device_count, dtype=jnp.int32)[:, None]
    target_row = (device_ids // PEERS + row_step) % CYCLE
    local_pick = jax.random.randint(jax.random.fold_in(key, 12), (device_count, tile_total), 0, BLK_DEV, dtype=jnp.int32)
    local_pick = jnp.where(slots == 0, 0, jnp.where(slots == tile_total - 1, BLK_DEV - 1, local_pick))
    source = (target_row * PEERS + peer_pick) * BLK_DEV + local_pick
    return source.reshape(BLOCKS, TILES).astype(jnp.int32)


def draw_tile_edges(key, part):
    level = jax.random.randint(jax.random.fold_in(key, 21), (BLOCKS, 1, BLOCK, 1), 0, 8, dtype=jnp.int32)
    draws = jax.random.randint(jax.random.fold_in(key, 22), (BLOCKS, TILES, BLOCK, BLOCK), 0, 1048576, dtype=jnp.int32)
    limit = jnp.right_shift(jnp.full(level.shape, 1048576, jnp.int32), level + 2)
    return jnp.where(draws < limit, 1.0, 0.0).astype(jnp.float32).astype(jnp.bfloat16)


def place_ends(array, key, least, high):
    longest = array.shape.index(max(array.shape))
    spots = []
    for shift in (0, 1):
        where = [jax.random.randint(jax.random.fold_in(key, axis), (), 0, length) for axis, length in enumerate(array.shape)]
        where[longest] = (where[longest] + shift) % array.shape[longest]
        spots.append(tuple(where))
    return array.at[spots[0]].set(least).at[spots[1]].set(high)


def steps_of(rng, dims, cuts, least, largest):
    loudness, own = 1.0, jax.random.fold_in(rng, 6)
    for dim, shards_of in cuts:
        steps = jnp.exp(jax.random.uniform(jax.random.fold_in(own, dim), (shards_of,), jnp.float32, least / len(cuts), largest / len(cuts)))
        loudness = loudness * jnp.repeat(steps, dims[dim] // shards_of).reshape([-1 if axis == dim else 1 for axis in range(len(dims))])
    return loudness


def centred(rng, extent, width, most, cuts=(), kind=jnp.bfloat16):
    array = jax.random.normal(rng, extent, jnp.float32) * width
    if len(cuts) > 0:
        array = steps_of(rng, extent, cuts, -0.22, 0.18) * array
    return jnp.clip(array, min=-most, max=most).astype(kind)


def setup_inputs(seed: int = 0) -> dict:
    streams_of = jax.random.split(jax.random.key(seed), 14)
    node_feats = centred(streams_of[0], (NODES, FEAT), 1.0, 6.0, ((0, 128),))
    history = centred(streams_of[1], (NODES, WIDTH), 1.0, 6.0, ((0, 128),))
    tile_src = draw_tile_src(jax.random.fold_in(streams_of[13], 71), 0)
    tile_count = place_ends(jax.random.randint(streams_of[3], (BLOCKS,), 1, TILES + 1), jax.random.fold_in(streams_of[3], 1), 1, TILES).astype(jnp.int32)
    tile_edges = draw_tile_edges(jax.random.fold_in(streams_of[13], 71), 0)
    w1_self = centred(streams_of[5], (FEAT, WIDTH), FEAT ** -0.5, 0.5)
    w1_nbr = centred(streams_of[6], (FEAT, WIDTH), FEAT ** -0.5, 0.5)
    bias_one = centred(streams_of[7], (WIDTH,), 0.5, 3.0, (), jnp.float32)
    gain_one = jnp.clip(1.0 + 0.1 * jax.random.normal(streams_of[8], (WIDTH,), jnp.float32), 0.5, 1.5)
    w2_self = centred(streams_of[9], (WIDTH, WIDTH), WIDTH ** -0.5, 0.1875)
    w2_nbr = centred(streams_of[10], (WIDTH, WIDTH), WIDTH ** -0.5, 0.1875)
    bias_two = centred(streams_of[11], (WIDTH,), 0.5, 3.0, (), jnp.float32)
    gain_two = jnp.clip(1.0 + 0.1 * jax.random.normal(streams_of[12], (WIDTH,), jnp.float32), 0.5, 1.5)
    return {"node_feats": node_feats, "history": history, "tile_src": tile_src, "tile_count": tile_count, "tile_edges": tile_edges, "w1_self": w1_self, "w1_nbr": w1_nbr, "bias_one": bias_one, "gain_one": gain_one, "w2_self": w2_self, "w2_nbr": w2_nbr, "bias_two": bias_two, "gain_two": gain_two}


def rms_relu(values, gain_row):
    inv_scale = lax.rsqrt(lax.optimization_barrier(jnp.mean(values * values, axis=-1, keepdims=True)) + 1e-06)
    return jax.nn.relu(values * inv_scale * gain_row).astype(jnp.bfloat16)

def sage_layer(self_rows, mean_rows, w_self, w_neighbour, bias_row, gain_row):
    summed = jnp.dot(self_rows, w_self, preferred_element_type=jnp.float32)
    summed = summed + jnp.dot(mean_rows, w_neighbour, preferred_element_type=jnp.float32)
    return rms_relu(summed + bias_row, gain_row)

def neighbour_means(table, tile_src, tile_count, tile_edges):
    blocks = table.reshape(BLOCKS, BLOCK, table.shape[1])

    def one_row(operands):
        row_edges, row_src, row_count = operands
        live_tiles = (jnp.arange(TILES, dtype=jnp.int32) < row_count).astype(row_edges.dtype)
        masked = row_edges * live_tiles[:, None, None]
        gathered = blocks[row_src]
        summed = jnp.einsum('tij,tjw->iw', masked.astype(jnp.float32), gathered.astype(jnp.float32))
        degree = jnp.maximum(lax.optimization_barrier(jnp.sum(masked.astype(jnp.float32), axis=(0, 2))), 1.0)
        return (summed / degree[:, None]).astype(jnp.bfloat16)
    averaged = lax.map(one_row, (tile_edges, tile_src, tile_count))
    return averaged.reshape(NODES, table.shape[1])

def reference(node_feats, history, tile_src, tile_count, tile_edges, w1_self, w1_nbr, bias_one, gain_one, w2_self, w2_nbr, bias_two, gain_two):
    mean_feats = neighbour_means(node_feats, tile_src, tile_count, tile_edges)
    mean_hist = neighbour_means(history, tile_src, tile_count, tile_edges)
    fresh_rows = sage_layer(node_feats, mean_feats, w1_self, w1_nbr, bias_one, gain_one)
    embed_rows = sage_layer(fresh_rows, mean_hist, w2_self, w2_nbr, bias_two, gain_two)
    return (fresh_rows, embed_rows)
```

```python
import functools

import jax
import jax.numpy as jnp
from jax import lax
from jax.experimental import pallas as pl
from jax.experimental.pallas import tpu as pltpu
from jax.sharding import PartitionSpec as P

MESH = pl.DeviceIdType.MESH
REGIONS = 8
SIDE = 4
PEERS = SIDE * SIDE
SLOTS = 2 * PEERS
BLOCK = 128
BLOCKS = 16
FEAT = 128
WIDTH = 1024
ROWS = BLOCKS * BLOCK
GROUPS = ((0, 256), (256, 256), (512, 256), (768, 128), (896, 128))
AHEAD = 3
BF16, F32 = jnp.bfloat16, jnp.float32


def rms_relu(values, gain_row):
    inv_scale = lax.rsqrt(jnp.mean(values * values, axis=-1, keepdims=True) + 1e-06)
    return jnp.maximum(values * inv_scale * gain_row, 0.0).astype(BF16)


def kernel(
    feats_hbm, hist_hbm, src_hbm, count_hbm, edges_hbm,
    w1s_hbm, w1n_hbm, bias_one_ref, gain_one_ref, w2s_hbm, w2n_hbm, bias_two_ref, gain_two_ref,
    fresh_ref, embed_ref,
    feats, hist, edges, w1, w2s, w2n, src, count, want, asked, ids,
    masked, scale, means, total,
    *rest,
):
    groups = 1 + len(GROUPS)
    sends, recvs = rest[:groups], rest[groups : 2 * groups]
    load_sem, req_send, req_recv, send_sem, recv_sem = rest[2 * groups :]
    region, me = lax.axis_index("blk"), lax.axis_index("narrow")
    my_y, my_z = me // SIDE, lax.rem(me, SIDE)
    behind, ahead = lax.rem(region + REGIONS - 1, REGIONS), lax.rem(region + 1, REGIONS)

    loads = [
        pltpu.make_async_copy(a, b, load_sem.at[i])
        for i, (a, b) in enumerate((
            (src_hbm, src), (count_hbm, count), (feats_hbm, feats), (hist_hbm, hist), (edges_hbm, edges),
            (w1s_hbm, w1.at[pl.ds(0, FEAT)]), (w1n_hbm, w1.at[pl.ds(FEAT, FEAT)]), (w2s_hbm, w2s), (w2n_hbm, w2n),
        ))
    ]
    for load in loads:
        load.start()

    barrier = pltpu.get_barrier_semaphore()

    def greet(k, _):
        other = lax.rem(me + k, PEERS)
        pl.semaphore_signal(barrier, inc=1, device_id=(behind, other), device_id_type=MESH)

        @pl.when(k > 0)
        def _():
            pl.semaphore_signal(barrier, inc=1, device_id=(region, other), device_id_type=MESH)

        return 0

    lax.fori_loop(0, PEERS, greet, 0)

    loads[0].wait()

    def slot_of(b, t):
        device = src[t, b] // BLOCKS
        step = lax.rem(device // PEERS - region + REGIONS, REGIONS)
        return jnp.minimum(step, 1) * PEERS + lax.rem(device, PEERS)

    lanes = lax.broadcasted_iota(jnp.int32, (1, 128), 1)
    wanted = jnp.zeros((1, 128), jnp.int32)
    for b in range(BLOCKS):
        for t in range(2):
            wanted = wanted + jnp.where(lanes == slot_of(b, t), lax.rem(src[t, b], BLOCKS), 0)
    want[...] = wanted
    asked[me] = wanted
    pl.semaphore_wait(barrier, SLOTS - 1)

    def ask(k, _):
        other = lax.rem(me + k, PEERS)

        def copy_to(blk, row):
            pltpu.make_async_remote_copy(
                src_ref=want, dst_ref=asked.at[row], send_sem=req_send, recv_sem=req_recv,
                device_id=(blk, other), device_id_type=MESH,
            ).start()

        copy_to(ahead, PEERS + me)

        @pl.when(k > 0)
        def _():
            copy_to(region, me)

        return 0

    lax.fori_loop(0, PEERS, ask, 0)
    all_asked = pltpu.make_async_remote_copy(
        src_ref=asked.at[pl.ds(0, SLOTS - 1)], dst_ref=asked.at[pl.ds(0, SLOTS - 1)],
        send_sem=req_send, recv_sem=req_recv, device_id=(region, lax.rem(me + 1, PEERS)), device_id_type=MESH,
    )
    all_asked.wait_recv()
    to_scalars = pltpu.make_async_copy(asked, ids, load_sem.at[len(loads)])
    to_scalars.start()
    to_scalars.wait()
    loads[2].wait()
    loads[3].wait()

    def picked(g, a):
        local = ids[a, 0, (a // PEERS) * PEERS + me]
        if g == 0:
            return feats[local]
        first, width = GROUPS[g - 1]
        return hist[local, :, first : first + width]

    def send_group(g):
        def step(k, blk, asker_region):
            place = lax.rem(5 * k, PEERS)
            y, z = lax.rem(my_y + place // SIDE, SIDE), lax.rem(my_z + place, SIDE)
            other = y * SIDE + z
            slot = asker_region * PEERS + other
            sends[g][slot] = picked(g, slot)
            pltpu.make_async_remote_copy(
                src_ref=sends[g].at[slot], dst_ref=recvs[g].at[asker_region * PEERS + me],
                send_sem=send_sem.at[g], recv_sem=recv_sem.at[g], device_id=(blk, other), device_id_type=MESH,
            ).start()

        def own(k, _):
            step(k, region, 0)
            return 0

        def previous(k, _):
            step(k, behind, 1)
            return 0

        lax.fori_loop(0, PEERS, previous, 0)
        lax.fori_loop(1, PEERS, own, 0)
        recvs[g][me] = picked(g, me)

    def whole(g):
        return pltpu.make_async_remote_copy(
            src_ref=sends[g].at[pl.ds(0, SLOTS - 1)], dst_ref=recvs[g].at[pl.ds(0, SLOTS - 1)],
            send_sem=send_sem.at[g], recv_sem=recv_sem.at[g],
            device_id=(region, lax.rem(me + 1, PEERS)), device_id_type=MESH,
        )

    for g in range(AHEAD):
        send_group(g)

    for load in loads[4:]:
        load.wait()
    loads[1].wait()

    def mask(b, _):
        for t in range(2):
            live = (t < count[b]).astype(F32)
            masked[b, :, t * BLOCK : (t + 1) * BLOCK] = (edges[b, t].astype(F32) * live).astype(BF16)
        degree = jnp.dot(masked[b], jnp.ones((2 * BLOCK, 128), BF16), preferred_element_type=F32)
        scale[b] = 1.0 / jnp.maximum(degree, 1.0)
        return 0

    lax.fori_loop(0, BLOCKS, mask, 0)

    def mean_of(g, b):
        pair = jnp.concatenate([recvs[g][slot_of(b, 0)], recvs[g][slot_of(b, 1)]], axis=0)
        summed = jnp.dot(masked[b], pair, preferred_element_type=F32)
        width = summed.shape[1]
        return (summed * jnp.concatenate([scale[b]] * (width // 128), axis=1)).astype(BF16)

    def average(g):
        width = recvs[g].shape[2]

        def one(b, _):
            means[pl.ds(pl.multiple_of(b * BLOCK, BLOCK), BLOCK), :width] = mean_of(g, b)
            return 0

        lax.fori_loop(0, BLOCKS, one, 0)

    whole(0).wait_recv()

    def layer_one(b, _):
        rows = pl.ds(pl.multiple_of(b * BLOCK, BLOCK), BLOCK)
        both = jnp.concatenate([feats[b], mean_of(0, b)], axis=1)
        z_one = jnp.dot(both, w1[...], preferred_element_type=F32) + bias_one_ref[...]
        fresh_ref[rows, :] = rms_relu(z_one, gain_one_ref[...])
        return 0

    lax.fori_loop(0, BLOCKS, layer_one, 0)
    TALL = 512

    def own_part(i, _):
        rows = pl.ds(pl.multiple_of(i * TALL, TALL), TALL)
        total[rows, :] = jnp.dot(fresh_ref[rows, :], w2s[...], preferred_element_type=F32) + bias_two_ref[...]
        return 0

    lax.fori_loop(0, ROWS // TALL, own_part, 0)

    for g in range(1, groups - 1):
        if g - 1 + AHEAD < groups:
            send_group(g - 1 + AHEAD)
        whole(g).wait_recv()
        average(g)
        first, width = GROUPS[g - 1]

        def add(i, _):
            rows = pl.ds(pl.multiple_of(i * TALL, TALL), TALL)
            total[rows, :] += jnp.dot(means[rows, :width], w2n[first : first + width, :], preferred_element_type=F32)
            return 0

        lax.fori_loop(0, ROWS // TALL, add, 0)

    g = groups - 1
    whole(g).wait_recv()
    first, width = GROUPS[g - 1]

    def finish(b, _):
        rows = pl.ds(pl.multiple_of(b * BLOCK, BLOCK), BLOCK)
        z_two = total[rows, :] + jnp.dot(mean_of(g, b), w2n[first : first + width, :], preferred_element_type=F32)
        embed_ref[rows, :] = rms_relu(z_two, gain_two_ref[...])
        return 0

    lax.fori_loop(0, BLOCKS, finish, 0)
    for g in range(groups):
        whole(g).wait_send()
    all_asked.wait_send()


def body(
    node_feats, history, tile_src, tile_count, tile_edges,
    w1_self, w1_nbr, bias_one, gain_one, w2_self, w2_nbr, bias_two, gain_two,
):
    widths = [FEAT] + [w for _, w in GROUPS]
    groups = len(widths)
    anywhere, vmem = pl.BlockSpec(memory_space=pl.ANY), pl.BlockSpec(memory_space=pltpu.VMEM)
    return pl.pallas_call(
        kernel,
        out_shape=(pltpu.VMEM((ROWS, WIDTH), BF16), pltpu.VMEM((ROWS, WIDTH), BF16)),
        in_specs=[anywhere] * 7 + [vmem] * 2 + [anywhere] * 2 + [vmem] * 2,
        out_specs=(vmem, vmem),
        scratch_shapes=[
            pltpu.VMEM((BLOCKS, BLOCK, FEAT), BF16),
            pltpu.VMEM((BLOCKS, BLOCK, WIDTH), BF16),
            pltpu.VMEM((BLOCKS, 2, BLOCK, BLOCK), BF16),
            pltpu.VMEM((2 * FEAT, WIDTH), BF16),
            pltpu.VMEM((WIDTH, WIDTH), BF16),
            pltpu.VMEM((WIDTH, WIDTH), BF16),
            pltpu.SMEM((2, BLOCKS), jnp.int32),
            pltpu.SMEM((BLOCKS,), jnp.int32),
            pltpu.VMEM((1, 128), jnp.int32),
            pltpu.VMEM((SLOTS, 1, 128), jnp.int32),
            pltpu.SMEM((SLOTS, 1, 128), jnp.int32),
            pltpu.VMEM((BLOCKS, BLOCK, 2 * BLOCK), BF16),
            pltpu.VMEM((BLOCKS, BLOCK, 128), F32),
            pltpu.VMEM((ROWS, 256), BF16),
            pltpu.VMEM((ROWS, WIDTH), F32),
        ]
        + [pltpu.VMEM((SLOTS, BLOCK, w), BF16) for w in widths] * 2
        + [
            pltpu.SemaphoreType.DMA((10,)),
            pltpu.SemaphoreType.DMA,
            pltpu.SemaphoreType.DMA,
            pltpu.SemaphoreType.DMA((groups,)),
            pltpu.SemaphoreType.DMA((groups,)),
        ],
        compiler_params=pltpu.CompilerParams(collective_id=0, has_side_effects=True, vmem_limit_bytes=48 << 20),
        name="sage",
    )(
        node_feats.reshape(BLOCKS, BLOCK, FEAT), history.reshape(BLOCKS, BLOCK, WIDTH), tile_src.T, tile_count,
        tile_edges, w1_self, w1_nbr, bias_one.reshape(1, WIDTH), gain_one.reshape(1, WIDTH), w2_self, w2_nbr,
        bias_two.reshape(1, WIDTH), gain_two.reshape(1, WIDTH),
    )


def solution(mesh):
    nodes = P(("blk", "narrow"), None)
    return jax.shard_map(
        body,
        mesh=mesh,
        in_specs=(nodes, nodes, nodes, P(("blk", "narrow")), P(("blk", "narrow"), None, None, None)) + (P(),) * 8,
        out_specs=(nodes, nodes),
        check_vma=False,
    )
```

```python
import functools

import jax
import jax.numpy as jnp
from jax import lax
from jax.experimental import pallas as pl
from jax.experimental.pallas import tpu as pltpu
from jax.sharding import PartitionSpec as P

MESH = pl.DeviceIdType.MESH
REGIONS = 8
SIDE = 4
PEERS = SIDE * SIDE
SLOTS = 2 * PEERS
BLOCK = 128
BLOCKS = 16
FEAT = 128
WIDTH = 1024
ROWS = BLOCKS * BLOCK
GROUPS = ((0, 256), (256, 256), (512, 256), (768, 128), (896, 128))
TALL = 512
AHEAD = 6
BF16, F32 = jnp.bfloat16, jnp.float32


def rms_relu(values, gain_row):
    inv_scale = lax.rsqrt(jnp.mean(values * values, axis=-1, keepdims=True) + 1e-06)
    return jnp.maximum(values * inv_scale * gain_row, 0.0).astype(BF16)


def kernel(
    feats_hbm, hist_hbm, src_hbm, count_hbm, edges_hbm,
    w1s_hbm, w1n_hbm, bias_one_hbm, gain_one_hbm, w2s_hbm, w2n_hbm, bias_two_hbm,
    fresh_ref, total, last_means, last_w2n,
    feats, hist, edges, w1, w2s, w2n, src, count, want, asked, ids,
    bias_one_ref, gain_one_ref, bias_two_ref, masked, scale, means,
    *rest,
):
    groups = 1 + len(GROUPS)
    sends, recvs = rest[:groups], rest[groups : 2 * groups]
    load_sem, req_send, req_recv, send_sem, recv_sem = rest[2 * groups :]
    region, me = lax.axis_index("blk"), lax.axis_index("narrow")
    my_y, my_z = me // SIDE, lax.rem(me, SIDE)
    behind, ahead = lax.rem(region + REGIONS - 1, REGIONS), lax.rem(region + 1, REGIONS)

    loads = [
        pltpu.make_async_copy(a, b, load_sem.at[i])
        for i, (a, b) in enumerate((
            (src_hbm, src), (count_hbm, count), (feats_hbm, feats), (hist_hbm, hist), (edges_hbm, edges),
            (w1s_hbm, w1.at[pl.ds(0, FEAT)]), (w1n_hbm, w1.at[pl.ds(FEAT, FEAT)]), (w2s_hbm, w2s), (w2n_hbm, w2n),
            (bias_one_hbm, bias_one_ref), (gain_one_hbm, gain_one_ref), (bias_two_hbm, bias_two_ref),
        ))
    ]
    for load in loads:
        load.start()

    barrier = pltpu.get_barrier_semaphore()

    def greet(k, _):
        other = lax.rem(me + k, PEERS)
        pl.semaphore_signal(barrier, inc=1, device_id=(behind, other), device_id_type=MESH)

        @pl.when(k > 0)
        def _():
            pl.semaphore_signal(barrier, inc=1, device_id=(region, other), device_id_type=MESH)

        return 0

    lax.fori_loop(0, PEERS, greet, 0)

    loads[0].wait()

    def slot_of(b, t):
        device = src[t, b] // BLOCKS
        step = lax.rem(device // PEERS - region + REGIONS, REGIONS)
        return jnp.minimum(step, 1) * PEERS + lax.rem(device, PEERS)

    lanes = lax.broadcasted_iota(jnp.int32, (1, 128), 1)
    wanted = jnp.zeros((1, 128), jnp.int32)
    for b in range(BLOCKS):
        for t in range(2):
            wanted = wanted + jnp.where(lanes == slot_of(b, t), lax.rem(src[t, b], BLOCKS), 0)
    want[...] = wanted
    asked[me] = wanted
    pl.semaphore_wait(barrier, SLOTS - 1)

    def ask(k, _):
        other = lax.rem(me + k, PEERS)

        def copy_to(blk, row):
            pltpu.make_async_remote_copy(
                src_ref=want, dst_ref=asked.at[row], send_sem=req_send, recv_sem=req_recv,
                device_id=(blk, other), device_id_type=MESH,
            ).start()

        copy_to(ahead, PEERS + me)

        @pl.when(k > 0)
        def _():
            copy_to(region, me)

        return 0

    lax.fori_loop(0, PEERS, ask, 0)
    all_asked = pltpu.make_async_remote_copy(
        src_ref=asked.at[pl.ds(0, SLOTS - 1)], dst_ref=asked.at[pl.ds(0, SLOTS - 1)],
        send_sem=req_send, recv_sem=req_recv, device_id=(region, lax.rem(me + 1, PEERS)), device_id_type=MESH,
    )
    all_asked.wait_recv()
    to_scalars = pltpu.make_async_copy(asked, ids, load_sem.at[len(loads)])
    to_scalars.start()
    to_scalars.wait()
    loads[2].wait()
    loads[3].wait()

    def picked(g, a):
        local = ids[a, 0, (a // PEERS) * PEERS + me]
        if g == 0:
            return feats[local]
        first, width = GROUPS[g - 1]
        return hist[local, :, first : first + width]

    def send_group(g):
        def step(k, blk, asker_region):
            place = lax.rem(5 * k, PEERS)
            y, z = lax.rem(my_y + place // SIDE, SIDE), lax.rem(my_z + place, SIDE)
            other = y * SIDE + z
            slot = asker_region * PEERS + other
            sends[g][slot] = picked(g, slot)
            pltpu.make_async_remote_copy(
                src_ref=sends[g].at[slot], dst_ref=recvs[g].at[asker_region * PEERS + me],
                send_sem=send_sem.at[g], recv_sem=recv_sem.at[g], device_id=(blk, other), device_id_type=MESH,
            ).start()

        def own(k, _):
            step(k, region, 0)
            return 0

        def previous(k, _):
            step(k, behind, 1)
            return 0

        lax.fori_loop(0, PEERS, previous, 0)
        lax.fori_loop(1, PEERS, own, 0)
        recvs[g][me] = picked(g, me)

    def whole(g):
        return pltpu.make_async_remote_copy(
            src_ref=sends[g].at[pl.ds(0, SLOTS - 1)], dst_ref=recvs[g].at[pl.ds(0, SLOTS - 1)],
            send_sem=send_sem.at[g], recv_sem=recv_sem.at[g],
            device_id=(region, lax.rem(me + 1, PEERS)), device_id_type=MESH,
        )

    for g in range(AHEAD):
        send_group(g)

    for load in loads[4:]:
        load.wait()
    loads[1].wait()

    def mask(b, _):
        for t in range(2):
            live = (t < count[b]).astype(F32)
            masked[b, :, t * BLOCK : (t + 1) * BLOCK] = (edges[b, t].astype(F32) * live).astype(BF16)
        degree = jnp.dot(masked[b], jnp.ones((2 * BLOCK, 128), BF16), preferred_element_type=F32)
        scale[b] = 1.0 / jnp.maximum(degree, 1.0)
        return 0

    lax.fori_loop(0, BLOCKS, mask, 0)

    def mean_of(g, b):
        pair = jnp.concatenate([recvs[g][slot_of(b, 0)], recvs[g][slot_of(b, 1)]], axis=0)
        summed = jnp.dot(masked[b], pair, preferred_element_type=F32)
        width = summed.shape[1]
        return (summed * jnp.concatenate([scale[b]] * (width // 128), axis=1)).astype(BF16)

    def average(g, means):
        width = recvs[g].shape[2]

        def one(b, _):
            means[pl.ds(pl.multiple_of(b * BLOCK, BLOCK), BLOCK), :width] = mean_of(g, b)
            return 0

        lax.fori_loop(0, BLOCKS, one, 0, unroll=4)

    whole(0).wait_recv()

    def layer_one(b, _):
        rows = pl.ds(pl.multiple_of(b * BLOCK, BLOCK), BLOCK)
        both = jnp.concatenate([feats[b], mean_of(0, b)], axis=1)
        z_one = jnp.dot(both, w1[...], preferred_element_type=F32) + bias_one_ref[...]
        fresh_ref[rows, :] = rms_relu(z_one, gain_one_ref[...])
        return 0

    lax.fori_loop(0, BLOCKS, layer_one, 0)
    def own_part(i, _):
        rows = pl.ds(pl.multiple_of(i * TALL, TALL), TALL)
        total[rows, :] = jnp.dot(fresh_ref[rows, :], w2s[...], preferred_element_type=F32) + bias_two_ref[...]
        return 0

    lax.fori_loop(0, ROWS // TALL, own_part, 0)

    for g in range(1, groups - 1):
        if g - 1 + AHEAD < groups:
            send_group(g - 1 + AHEAD)
        whole(g).wait_recv()
        average(g, means)
        first, width = GROUPS[g - 1]

        def add(i, _):
            rows = pl.ds(pl.multiple_of(i * TALL, TALL), TALL)
            total[rows, :] += jnp.dot(means[rows, :width], w2n[first : first + width, :], preferred_element_type=F32)
            return 0

        lax.fori_loop(0, ROWS // TALL, add, 0)

    g = groups - 1
    first, width = GROUPS[g - 1]
    last_w2n[...] = w2n[first : first + width, :]
    whole(g).wait_recv()
    average(g, last_means)
    for g in range(groups):
        whole(g).wait_send()
    all_asked.wait_send()


def finish(total, means, w2n, fresh, gain_ref, fresh_hbm, embed_hbm, staged, sems):
    pass_on = pltpu.make_async_copy(fresh, fresh_hbm, sems.at[0])
    pass_on.start()

    def step(i, _):
        rows = pl.ds(pl.multiple_of(i * TALL, TALL), TALL)
        z_two = total[rows, :] + jnp.dot(means[rows, :], w2n[...], preferred_element_type=F32)
        staged[rows, :] = rms_relu(z_two, gain_ref[...])
        pltpu.make_async_copy(staged.at[rows], embed_hbm.at[rows], sems.at[1]).start()
        return 0

    lax.fori_loop(0, ROWS // TALL, step, 0)
    pltpu.make_async_copy(staged, embed_hbm, sems.at[1]).wait()
    pass_on.wait()


def body(
    node_feats, history, tile_src, tile_count, tile_edges,
    w1_self, w1_nbr, bias_one, gain_one, w2_self, w2_nbr, bias_two, gain_two,
):
    widths = [FEAT] + [w for _, w in GROUPS]
    groups = len(widths)
    hbm, vmem = pl.BlockSpec(memory_space=pltpu.HBM), pl.BlockSpec(memory_space=pltpu.VMEM)
    last = widths[-1]
    operands = (
        node_feats.reshape(BLOCKS, BLOCK, FEAT), history.reshape(BLOCKS, BLOCK, WIDTH), tile_src.T, tile_count,
        tile_edges, w1_self, w1_nbr, bias_one.reshape(1, WIDTH), gain_one.reshape(1, WIDTH), w2_self, w2_nbr,
        bias_two.reshape(1, WIDTH),
    )
    fresh, total, means, w2n_rows = pl.pallas_call(
        kernel,
        out_shape=(
            pltpu.VMEM((ROWS, WIDTH), BF16),
            pltpu.VMEM((ROWS, WIDTH), F32),
            pltpu.VMEM((ROWS, last), BF16),
            pltpu.VMEM((last, WIDTH), BF16),
        ),
        in_specs=[hbm] * 12,
        out_specs=(vmem,) * 4,
        scratch_shapes=[
            pltpu.VMEM((BLOCKS, BLOCK, FEAT), BF16),
            pltpu.VMEM((BLOCKS, BLOCK, WIDTH), BF16),
            pltpu.VMEM((BLOCKS, 2, BLOCK, BLOCK), BF16),
            pltpu.VMEM((2 * FEAT, WIDTH), BF16),
            pltpu.VMEM((WIDTH, WIDTH), BF16),
            pltpu.VMEM((WIDTH, WIDTH), BF16),
            pltpu.SMEM((2, BLOCKS), jnp.int32),
            pltpu.SMEM((BLOCKS,), jnp.int32),
            pltpu.VMEM((1, 128), jnp.int32),
            pltpu.VMEM((SLOTS, 1, 128), jnp.int32),
            pltpu.SMEM((SLOTS, 1, 128), jnp.int32),
            pltpu.VMEM((1, WIDTH), F32),
            pltpu.VMEM((1, WIDTH), F32),
            pltpu.VMEM((1, WIDTH), F32),
            pltpu.VMEM((BLOCKS, BLOCK, 2 * BLOCK), BF16),
            pltpu.VMEM((BLOCKS, BLOCK, 128), F32),
            pltpu.VMEM((ROWS, 256), BF16),
        ]
        + [pltpu.VMEM((SLOTS, BLOCK, w), BF16) for w in widths] * 2
        + [
            pltpu.SemaphoreType.DMA((13,)),
            pltpu.SemaphoreType.DMA,
            pltpu.SemaphoreType.DMA,
            pltpu.SemaphoreType.DMA((groups,)),
            pltpu.SemaphoreType.DMA((groups,)),
        ],
        compiler_params=pltpu.CompilerParams(collective_id=0, has_side_effects=True, vmem_limit_bytes=40 << 20),
        name="sage",
    )(
        *(pltpu.with_memory_space_constraint(a, pltpu.HBM) for a in operands)
    )
    rows = jax.ShapeDtypeStruct((ROWS, WIDTH), BF16)
    return pl.pallas_call(
        finish,
        out_shape=(rows, rows),
        in_specs=[vmem] * 5,
        out_specs=(hbm,) * 2,
        scratch_shapes=[pltpu.VMEM((ROWS, WIDTH), BF16), pltpu.SemaphoreType.DMA((2,))],
        compiler_params=pltpu.CompilerParams(vmem_limit_bytes=12 << 20),
        name="finish",
    )(total, means, w2n_rows, fresh, gain_two.reshape(1, WIDTH))


def solution(mesh):
    nodes = P(("blk", "narrow"), None)
    return jax.shard_map(
        body,
        mesh=mesh,
        in_specs=(nodes, nodes, nodes, P(("blk", "narrow")), P(("blk", "narrow"), None, None, None)) + (P(),) * 8,
        out_specs=(nodes, nodes),
        check_vma=False,
    )
```

```python
import functools

import jax
import jax.numpy as jnp
from jax import lax
from jax.experimental import pallas as pl
from jax.experimental.pallas import tpu as pltpu
from jax.sharding import PartitionSpec as P

MESH = pl.DeviceIdType.MESH
REGIONS = 8
SIDE = 4
PEERS = SIDE * SIDE
SLOTS = 2 * PEERS
BLOCK = 128
BLOCKS = 16
FEAT = 128
WIDTH = 1024
ROWS = BLOCKS * BLOCK
GROUPS = ((0, 256), (256, 256), (512, 256), (768, 128), (896, 128))
TALL = 512
AHEAD = 6
BF16, F32 = jnp.bfloat16, jnp.float32


def rms_relu(values, gain_row):
    inv_scale = lax.rsqrt(jnp.mean(values * values, axis=-1, keepdims=True) + 1e-06)
    return jnp.maximum(values * inv_scale * gain_row, 0.0).astype(BF16)


def kernel(
    feats_hbm, hist_hbm, src_hbm, count_hbm, edges_hbm,
    w1s_hbm, w1n_hbm, bias_one_hbm, gain_one_hbm, w2s_hbm, w2n_hbm, bias_two_hbm,
    fresh_ref, total, last_means, last_w2n,
    feats, hist, edges, w1, w2s, w2n, src, count, want, asked, ids,
    bias_one_ref, gain_one_ref, bias_two_ref, masked, scale, means,
    *rest,
):
    groups = 1 + len(GROUPS)
    sends, recvs = rest[:groups], rest[groups : 2 * groups]
    load_sem, req_send, req_recv, send_sem, recv_sem = rest[2 * groups :]
    region, me = lax.axis_index("blk"), lax.axis_index("narrow")
    my_y, my_z = me // SIDE, lax.rem(me, SIDE)
    behind, ahead = lax.rem(region + REGIONS - 1, REGIONS), lax.rem(region + 1, REGIONS)

    loads = [
        pltpu.make_async_copy(a, b, load_sem.at[i])
        for i, (a, b) in enumerate((
            (src_hbm, src), (count_hbm, count), (feats_hbm, feats), (hist_hbm, hist), (edges_hbm, edges),
            (w1s_hbm, w1.at[pl.ds(0, FEAT)]), (w1n_hbm, w1.at[pl.ds(FEAT, FEAT)]), (w2s_hbm, w2s), (w2n_hbm, w2n),
            (bias_one_hbm, bias_one_ref), (gain_one_hbm, gain_one_ref), (bias_two_hbm, bias_two_ref),
        ))
    ]
    for load in loads:
        load.start()

    barrier = pltpu.get_barrier_semaphore()

    def greet(k, _):
        other = lax.rem(me + k, PEERS)
        pl.semaphore_signal(barrier, inc=1, device_id=(behind, other), device_id_type=MESH)

        @pl.when(k > 0)
        def _():
            pl.semaphore_signal(barrier, inc=1, device_id=(region, other), device_id_type=MESH)

        return 0

    lax.fori_loop(0, PEERS, greet, 0)

    loads[0].wait()

    def slot_of(b, t):
        device = src[t, b] // BLOCKS
        step = lax.rem(device // PEERS - region + REGIONS, REGIONS)
        return jnp.minimum(step, 1) * PEERS + lax.rem(device, PEERS)

    lanes = lax.broadcasted_iota(jnp.int32, (1, 128), 1)
    wanted = jnp.zeros((1, 128), jnp.int32)
    for b in range(BLOCKS):
        for t in range(2):
            wanted = wanted + jnp.where(lanes == slot_of(b, t), lax.rem(src[t, b], BLOCKS), 0)
    want[...] = wanted
    asked[me] = wanted
    pl.semaphore_wait(barrier, SLOTS - 1)

    def ask(k, _):
        other = lax.rem(me + k, PEERS)

        def copy_to(blk, row):
            pltpu.make_async_remote_copy(
                src_ref=want, dst_ref=asked.at[row], send_sem=req_send, recv_sem=req_recv,
                device_id=(blk, other), device_id_type=MESH,
            ).start()

        copy_to(ahead, PEERS + me)

        @pl.when(k > 0)
        def _():
            copy_to(region, me)

        return 0

    lax.fori_loop(0, PEERS, ask, 0)
    all_asked = pltpu.make_async_remote_copy(
        src_ref=asked.at[pl.ds(0, SLOTS - 1)], dst_ref=asked.at[pl.ds(0, SLOTS - 1)],
        send_sem=req_send, recv_sem=req_recv, device_id=(region, lax.rem(me + 1, PEERS)), device_id_type=MESH,
    )
    all_asked.wait_recv()
    to_scalars = pltpu.make_async_copy(asked, ids, load_sem.at[len(loads)])
    to_scalars.start()
    to_scalars.wait()
    loads[2].wait()
    loads[3].wait()

    def picked(g, a):
        local = ids[a, 0, (a // PEERS) * PEERS + me]
        if g == 0:
            return feats[local]
        first, width = GROUPS[g - 1]
        return hist[local, :, first : first + width]

    def send_group(g):
        def step(k, blk, asker_region):
            place = lax.rem(5 * k, PEERS)
            y, z = lax.rem(my_y + place // SIDE, SIDE), lax.rem(my_z + place, SIDE)
            other = y * SIDE + z
            slot = asker_region * PEERS + other
            sends[g][slot] = picked(g, slot)
            pltpu.make_async_remote_copy(
                src_ref=sends[g].at[slot], dst_ref=recvs[g].at[asker_region * PEERS + me],
                send_sem=send_sem.at[g], recv_sem=recv_sem.at[g], device_id=(blk, other), device_id_type=MESH,
            ).start()

        def own(k, _):
            step(k, region, 0)
            return 0

        def previous(k, _):
            step(k, behind, 1)
            return 0

        lax.fori_loop(1, PEERS, own, 0)
        lax.fori_loop(0, PEERS, previous, 0)
        recvs[g][me] = picked(g, me)

    def whole(g):
        return pltpu.make_async_remote_copy(
            src_ref=sends[g].at[pl.ds(0, SLOTS - 1)], dst_ref=recvs[g].at[pl.ds(0, SLOTS - 1)],
            send_sem=send_sem.at[g], recv_sem=recv_sem.at[g],
            device_id=(region, lax.rem(me + 1, PEERS)), device_id_type=MESH,
        )

    for g in range(AHEAD):
        send_group(g)

    for load in loads[4:]:
        load.wait()
    loads[1].wait()

    def mask(b, _):
        for t in range(2):
            live = (t < count[b]).astype(F32)
            masked[b, :, t * BLOCK : (t + 1) * BLOCK] = (edges[b, t].astype(F32) * live).astype(BF16)
        degree = jnp.dot(masked[b], jnp.ones((2 * BLOCK, 128), BF16), preferred_element_type=F32)
        scale[b] = 1.0 / jnp.maximum(degree, 1.0)
        return 0

    lax.fori_loop(0, BLOCKS, mask, 0)

    def mean_of(g, b):
        pair = jnp.concatenate([recvs[g][slot_of(b, 0)], recvs[g][slot_of(b, 1)]], axis=0)
        summed = jnp.dot(masked[b], pair, preferred_element_type=F32)
        width = summed.shape[1]
        return (summed * jnp.concatenate([scale[b]] * (width // 128), axis=1)).astype(BF16)

    def average(g, means):
        width = recvs[g].shape[2]

        def one(b, _):
            means[pl.ds(pl.multiple_of(b * BLOCK, BLOCK), BLOCK), :width] = mean_of(g, b)
            return 0

        lax.fori_loop(0, BLOCKS, one, 0, unroll=4)

    whole(0).wait_recv()

    def layer_one(b, _):
        rows = pl.ds(pl.multiple_of(b * BLOCK, BLOCK), BLOCK)
        both = jnp.concatenate([feats[b], mean_of(0, b)], axis=1)
        z_one = jnp.dot(both, w1[...], preferred_element_type=F32) + bias_one_ref[...]
        fresh_ref[rows, :] = rms_relu(z_one, gain_one_ref[...])
        return 0

    lax.fori_loop(0, BLOCKS, layer_one, 0)
    def own_part(i, _):
        rows = pl.ds(pl.multiple_of(i * TALL, TALL), TALL)
        total[rows, :] = jnp.dot(fresh_ref[rows, :], w2s[...], preferred_element_type=F32) + bias_two_ref[...]
        return 0

    lax.fori_loop(0, ROWS // TALL, own_part, 0)

    for g in range(1, groups - 1):
        if g - 1 + AHEAD < groups:
            send_group(g - 1 + AHEAD)
        whole(g).wait_recv()
        average(g, means)
        first, width = GROUPS[g - 1]

        def add(i, _):
            rows = pl.ds(pl.multiple_of(i * TALL, TALL), TALL)
            total[rows, :] += jnp.dot(means[rows, :width], w2n[first : first + width, :], preferred_element_type=F32)
            return 0

        lax.fori_loop(0, ROWS // TALL, add, 0)

    g = groups - 1
    first, width = GROUPS[g - 1]
    last_w2n[...] = w2n[first : first + width, :]
    whole(g).wait_recv()
    average(g, last_means)
    for g in range(groups):
        whole(g).wait_send()
    all_asked.wait_send()


def finish(total, means, w2n, fresh, gain_ref, fresh_hbm, embed_hbm, staged, sems):
    pass_on = pltpu.make_async_copy(fresh, fresh_hbm, sems.at[0])
    pass_on.start()

    def step(i, _):
        rows = pl.ds(pl.multiple_of(i * TALL, TALL), TALL)
        z_two = total[rows, :] + jnp.dot(means[rows, :], w2n[...], preferred_element_type=F32)
        staged[rows, :] = rms_relu(z_two, gain_ref[...])
        pltpu.make_async_copy(staged.at[rows], embed_hbm.at[rows], sems.at[1]).start()
        return 0

    lax.fori_loop(0, ROWS // TALL, step, 0, unroll=True)
    pltpu.make_async_copy(staged, embed_hbm, sems.at[1]).wait()
    pass_on.wait()


def body(
    node_feats, history, tile_src, tile_count, tile_edges,
    w1_self, w1_nbr, bias_one, gain_one, w2_self, w2_nbr, bias_two, gain_two,
):
    widths = [FEAT] + [w for _, w in GROUPS]
    groups = len(widths)
    hbm, vmem = pl.BlockSpec(memory_space=pltpu.HBM), pl.BlockSpec(memory_space=pltpu.VMEM)
    last = widths[-1]
    operands = (
        node_feats.reshape(BLOCKS, BLOCK, FEAT), history.reshape(BLOCKS, BLOCK, WIDTH), tile_src.T, tile_count,
        tile_edges, w1_self, w1_nbr, bias_one.reshape(1, WIDTH), gain_one.reshape(1, WIDTH), w2_self, w2_nbr,
        bias_two.reshape(1, WIDTH),
    )
    fresh, total, means, w2n_rows = pl.pallas_call(
        kernel,
        out_shape=(
            pltpu.VMEM((ROWS, WIDTH), BF16),
            pltpu.VMEM((ROWS, WIDTH), F32),
            pltpu.VMEM((ROWS, last), BF16),
            pltpu.VMEM((last, WIDTH), BF16),
        ),
        in_specs=[hbm] * 12,
        out_specs=(vmem,) * 4,
        scratch_shapes=[
            pltpu.VMEM((BLOCKS, BLOCK, FEAT), BF16),
            pltpu.VMEM((BLOCKS, BLOCK, WIDTH), BF16),
            pltpu.VMEM((BLOCKS, 2, BLOCK, BLOCK), BF16),
            pltpu.VMEM((2 * FEAT, WIDTH), BF16),
            pltpu.VMEM((WIDTH, WIDTH), BF16),
            pltpu.VMEM((WIDTH, WIDTH), BF16),
            pltpu.SMEM((2, BLOCKS), jnp.int32),
            pltpu.SMEM((BLOCKS,), jnp.int32),
            pltpu.VMEM((1, 128), jnp.int32),
            pltpu.VMEM((SLOTS, 1, 128), jnp.int32),
            pltpu.SMEM((SLOTS, 1, 128), jnp.int32),
            pltpu.VMEM((1, WIDTH), F32),
            pltpu.VMEM((1, WIDTH), F32),
            pltpu.VMEM((1, WIDTH), F32),
            pltpu.VMEM((BLOCKS, BLOCK, 2 * BLOCK), BF16),
            pltpu.VMEM((BLOCKS, BLOCK, 128), F32),
            pltpu.VMEM((ROWS, 256), BF16),
        ]
        + [pltpu.VMEM((SLOTS, BLOCK, w), BF16) for w in widths] * 2
        + [
            pltpu.SemaphoreType.DMA((13,)),
            pltpu.SemaphoreType.DMA,
            pltpu.SemaphoreType.DMA,
            pltpu.SemaphoreType.DMA((groups,)),
            pltpu.SemaphoreType.DMA((groups,)),
        ],
        compiler_params=pltpu.CompilerParams(collective_id=0, has_side_effects=True, vmem_limit_bytes=40 << 20),
        name="sage",
    )(
        *(pltpu.with_memory_space_constraint(a, pltpu.HBM) for a in operands)
    )
    rows = jax.ShapeDtypeStruct((ROWS, WIDTH), BF16)
    return pl.pallas_call(
        finish,
        out_shape=(rows, rows),
        in_specs=[vmem] * 5,
        out_specs=(hbm,) * 2,
        scratch_shapes=[pltpu.VMEM((ROWS, WIDTH), BF16), pltpu.SemaphoreType.DMA((2,))],
        compiler_params=pltpu.CompilerParams(vmem_limit_bytes=12 << 20),
        name="finish",
    )(total, means, w2n_rows, fresh, gain_two.reshape(1, WIDTH))


def solution(mesh):
    nodes = P(("blk", "narrow"), None)
    return jax.shard_map(
        body,
        mesh=mesh,
        in_specs=(nodes, nodes, nodes, P(("blk", "narrow")), P(("blk", "narrow"), None, None, None)) + (P(),) * 8,
        out_specs=(nodes, nodes),
        check_vma=False,
    )
```

```python
import functools

import jax
import jax.numpy as jnp
from jax import lax
from jax.experimental import pallas as pl
from jax.experimental.pallas import tpu as pltpu
from jax.sharding import PartitionSpec as P

MESH = pl.DeviceIdType.MESH
REGIONS = 8
SIDE = 4
PEERS = SIDE * SIDE
SLOTS = 2 * PEERS
BLOCK = 128
BLOCKS = 16
FEAT = 128
WIDTH = 1024
ROWS = BLOCKS * BLOCK
GROUPS = ((0, 256), (256, 256), (512, 256), (768, 128), (896, 128))
TALL = 512
AHEAD = 6
BF16, F32 = jnp.bfloat16, jnp.float32


def rms_relu(values, gain_row):
    inv_scale = lax.rsqrt(jnp.mean(values * values, axis=-1, keepdims=True) + 1e-06)
    return jnp.maximum(values * inv_scale * gain_row, 0.0).astype(BF16)


def kernel(
    feats_hbm, hist_hbm, src_hbm, count_hbm, edges_hbm,
    w1s_hbm, w1n_hbm, bias_one_hbm, gain_one_hbm, w2s_hbm, w2n_hbm, bias_two_hbm,
    fresh_ref, total, last_means, last_w2n,
    feats, hist, edges, w1, w2s, w2n, src, count, want, asked, ids,
    bias_one_ref, gain_one_ref, bias_two_ref, masked, scale, means,
    *rest,
):
    groups = 1 + len(GROUPS)
    sends, recvs = rest[:groups], rest[groups : 2 * groups]
    load_sem, req_send, req_recv, send_sem, recv_sem = rest[2 * groups :]
    region, me = lax.axis_index("blk"), lax.axis_index("narrow")
    my_y, my_z = me // SIDE, lax.rem(me, SIDE)
    behind, ahead = lax.rem(region + REGIONS - 1, REGIONS), lax.rem(region + 1, REGIONS)

    loads = [
        pltpu.make_async_copy(a, b, load_sem.at[i])
        for i, (a, b) in enumerate((
            (src_hbm, src), (count_hbm, count), (feats_hbm, feats), (hist_hbm, hist), (edges_hbm, edges),
            (w1s_hbm, w1.at[pl.ds(0, FEAT)]), (w1n_hbm, w1.at[pl.ds(FEAT, FEAT)]), (w2s_hbm, w2s), (w2n_hbm, w2n),
            (bias_one_hbm, bias_one_ref), (gain_one_hbm, gain_one_ref), (bias_two_hbm, bias_two_ref),
        ))
    ]
    for load in loads:
        load.start()

    barrier = pltpu.get_barrier_semaphore()

    def greet(k, _):
        other = lax.rem(me + k, PEERS)
        pl.semaphore_signal(barrier, inc=1, device_id=(behind, other), device_id_type=MESH)

        @pl.when(k > 0)
        def _():
            pl.semaphore_signal(barrier, inc=1, device_id=(region, other), device_id_type=MESH)

        return 0

    lax.fori_loop(0, PEERS, greet, 0)

    loads[0].wait()

    def slot_of(b, t):
        device = src[t, b] // BLOCKS
        step = lax.rem(device // PEERS - region + REGIONS, REGIONS)
        return jnp.minimum(step, 1) * PEERS + lax.rem(device, PEERS)

    lanes = lax.broadcasted_iota(jnp.int32, (1, 128), 1)
    wanted = jnp.zeros((1, 128), jnp.int32)
    for b in range(BLOCKS):
        for t in range(2):
            wanted = wanted + jnp.where(lanes == slot_of(b, t), lax.rem(src[t, b], BLOCKS), 0)
    want[...] = wanted
    asked[me] = wanted
    pl.semaphore_wait(barrier, SLOTS - 1)

    def ask(k, _):
        place = lax.rem(14 + 15 * k, PEERS)
        other = lax.rem(my_y + place // SIDE, SIDE) * SIDE + lax.rem(my_z + place, SIDE)

        def copy_to(blk, row):
            pltpu.make_async_remote_copy(
                src_ref=want, dst_ref=asked.at[row], send_sem=req_send, recv_sem=req_recv,
                device_id=(blk, other), device_id_type=MESH,
            ).start()

        copy_to(ahead, PEERS + me)

        @pl.when(place > 0)
        def _():
            copy_to(region, me)

        return 0

    lax.fori_loop(0, PEERS, ask, 0)
    all_asked = pltpu.make_async_remote_copy(
        src_ref=asked.at[pl.ds(0, SLOTS - 1)], dst_ref=asked.at[pl.ds(0, SLOTS - 1)],
        send_sem=req_send, recv_sem=req_recv, device_id=(region, lax.rem(me + 1, PEERS)), device_id_type=MESH,
    )
    all_asked.wait_recv()
    to_scalars = pltpu.make_async_copy(asked, ids, load_sem.at[len(loads)])
    to_scalars.start()
    to_scalars.wait()
    loads[2].wait()
    loads[3].wait()

    def picked(g, a):
        local = ids[a, 0, (a // PEERS) * PEERS + me]
        if g == 0:
            return feats[local]
        first, width = GROUPS[g - 1]
        return hist[local, :, first : first + width]

    def send_group(g):
        def step(k, blk, asker_region):
            place = lax.rem(5 * k, PEERS)
            y, z = lax.rem(my_y + place // SIDE, SIDE), lax.rem(my_z + place, SIDE)
            other = y * SIDE + z
            slot = asker_region * PEERS + other
            sends[g][slot] = picked(g, slot)
            pltpu.make_async_remote_copy(
                src_ref=sends[g].at[slot], dst_ref=recvs[g].at[asker_region * PEERS + me],
                send_sem=send_sem.at[g], recv_sem=recv_sem.at[g], device_id=(blk, other), device_id_type=MESH,
            ).start()

        def own(k, _):
            step(k, region, 0)
            return 0

        def previous(k, _):
            step(k, behind, 1)
            return 0

        lax.fori_loop(1, PEERS, own, 0)
        lax.fori_loop(0, PEERS, previous, 0)
        recvs[g][me] = picked(g, me)

    def whole(g):
        return pltpu.make_async_remote_copy(
            src_ref=sends[g].at[pl.ds(0, SLOTS - 1)], dst_ref=recvs[g].at[pl.ds(0, SLOTS - 1)],
            send_sem=send_sem.at[g], recv_sem=recv_sem.at[g],
            device_id=(region, lax.rem(me + 1, PEERS)), device_id_type=MESH,
        )

    for g in range(AHEAD):
        send_group(g)

    for load in loads[4:]:
        load.wait()
    loads[1].wait()

    def mask(b, _):
        for t in range(2):
            live = (t < count[b]).astype(F32)
            masked[b, :, t * BLOCK : (t + 1) * BLOCK] = (edges[b, t].astype(F32) * live).astype(BF16)
        degree = jnp.dot(masked[b], jnp.ones((2 * BLOCK, 128), BF16), preferred_element_type=F32)
        scale[b] = 1.0 / jnp.maximum(degree, 1.0)
        return 0

    lax.fori_loop(0, BLOCKS, mask, 0)

    def mean_of(g, b):
        pair = jnp.concatenate([recvs[g][slot_of(b, 0)], recvs[g][slot_of(b, 1)]], axis=0)
        summed = jnp.dot(masked[b], pair, preferred_element_type=F32)
        width = summed.shape[1]
        return (summed * jnp.concatenate([scale[b]] * (width // 128), axis=1)).astype(BF16)

    def average(g, means, together):
        width = recvs[g].shape[2]

        def one(b, _):
            means[pl.ds(pl.multiple_of(b * BLOCK, BLOCK), BLOCK), :width] = mean_of(g, b)
            return 0

        lax.fori_loop(0, BLOCKS, one, 0, unroll=together)

    whole(0).wait_recv()

    def layer_one(b, _):
        rows = pl.ds(pl.multiple_of(b * BLOCK, BLOCK), BLOCK)
        both = jnp.concatenate([feats[b], mean_of(0, b)], axis=1)
        z_one = jnp.dot(both, w1[...], preferred_element_type=F32) + bias_one_ref[...]
        fresh_ref[rows, :] = rms_relu(z_one, gain_one_ref[...])
        return 0

    lax.fori_loop(0, BLOCKS, layer_one, 0)
    def own_part(i, _):
        rows = pl.ds(pl.multiple_of(i * TALL, TALL), TALL)
        total[rows, :] = jnp.dot(fresh_ref[rows, :], w2s[...], preferred_element_type=F32) + bias_two_ref[...]
        return 0

    lax.fori_loop(0, ROWS // TALL, own_part, 0)

    for g in range(1, groups - 1):
        if g - 1 + AHEAD < groups:
            send_group(g - 1 + AHEAD)
        whole(g).wait_recv()
        average(g, means, 4)
        first, width = GROUPS[g - 1]

        def add(i, _):
            rows = pl.ds(pl.multiple_of(i * TALL, TALL), TALL)
            total[rows, :] += jnp.dot(means[rows, :width], w2n[first : first + width, :], preferred_element_type=F32)
            return 0

        lax.fori_loop(0, ROWS // TALL, add, 0)

    g = groups - 1
    first, width = GROUPS[g - 1]
    last_w2n[...] = w2n[first : first + width, :]
    whole(g).wait_recv()
    average(g, last_means, BLOCKS)
    for g in range(groups):
        whole(g).wait_send()
    all_asked.wait_send()


def finish(total, means, w2n, fresh, gain_ref, fresh_hbm, embed_hbm, staged, sems):
    pass_on = pltpu.make_async_copy(fresh, fresh_hbm, sems.at[0])
    pass_on.start()

    def step(i, _):
        rows = pl.ds(pl.multiple_of(i * TALL, TALL), TALL)
        z_two = total[rows, :] + jnp.dot(means[rows, :], w2n[...], preferred_element_type=F32)
        staged[rows, :] = rms_relu(z_two, gain_ref[...])
        pltpu.make_async_copy(staged.at[rows], embed_hbm.at[rows], sems.at[1]).start()
        return 0

    lax.fori_loop(0, ROWS // TALL, step, 0, unroll=True)
    pltpu.make_async_copy(staged, embed_hbm, sems.at[1]).wait()
    pass_on.wait()


def body(
    node_feats, history, tile_src, tile_count, tile_edges,
    w1_self, w1_nbr, bias_one, gain_one, w2_self, w2_nbr, bias_two, gain_two,
):
    widths = [FEAT] + [w for _, w in GROUPS]
    groups = len(widths)
    hbm, vmem = pl.BlockSpec(memory_space=pltpu.HBM), pl.BlockSpec(memory_space=pltpu.VMEM)
    last = widths[-1]
    operands = (
        node_feats.reshape(BLOCKS, BLOCK, FEAT), history.reshape(BLOCKS, BLOCK, WIDTH), tile_src.T, tile_count,
        tile_edges, w1_self, w1_nbr, bias_one.reshape(1, WIDTH), gain_one.reshape(1, WIDTH), w2_self, w2_nbr,
        bias_two.reshape(1, WIDTH),
    )
    fresh, total, means, w2n_rows = pl.pallas_call(
        kernel,
        out_shape=(
            pltpu.VMEM((ROWS, WIDTH), BF16),
            pltpu.VMEM((ROWS, WIDTH), F32),
            pltpu.VMEM((ROWS, last), BF16),
            pltpu.VMEM((last, WIDTH), BF16),
        ),
        in_specs=[hbm] * 12,
        out_specs=(vmem,) * 4,
        scratch_shapes=[
            pltpu.VMEM((BLOCKS, BLOCK, FEAT), BF16),
            pltpu.VMEM((BLOCKS, BLOCK, WIDTH), BF16),
            pltpu.VMEM((BLOCKS, 2, BLOCK, BLOCK), BF16),
            pltpu.VMEM((2 * FEAT, WIDTH), BF16),
            pltpu.VMEM((WIDTH, WIDTH), BF16),
            pltpu.VMEM((WIDTH, WIDTH), BF16),
            pltpu.SMEM((2, BLOCKS), jnp.int32),
            pltpu.SMEM((BLOCKS,), jnp.int32),
            pltpu.VMEM((1, 128), jnp.int32),
            pltpu.VMEM((SLOTS, 1, 128), jnp.int32),
            pltpu.SMEM((SLOTS, 1, 128), jnp.int32),
            pltpu.VMEM((1, WIDTH), F32),
            pltpu.VMEM((1, WIDTH), F32),
            pltpu.VMEM((1, WIDTH), F32),
            pltpu.VMEM((BLOCKS, BLOCK, 2 * BLOCK), BF16),
            pltpu.VMEM((BLOCKS, BLOCK, 128), F32),
            pltpu.VMEM((ROWS, 256), BF16),
        ]
        + [pltpu.VMEM((SLOTS, BLOCK, w), BF16) for w in widths] * 2
        + [
            pltpu.SemaphoreType.DMA((13,)),
            pltpu.SemaphoreType.DMA,
            pltpu.SemaphoreType.DMA,
            pltpu.SemaphoreType.DMA((groups,)),
            pltpu.SemaphoreType.DMA((groups,)),
        ],
        compiler_params=pltpu.CompilerParams(collective_id=0, has_side_effects=True, vmem_limit_bytes=40 << 20),
        name="sage",
    )(
        *(pltpu.with_memory_space_constraint(a, pltpu.HBM) for a in operands)
    )
    rows = jax.ShapeDtypeStruct((ROWS, WIDTH), BF16)
    return pl.pallas_call(
        finish,
        out_shape=(rows, rows),
        in_specs=[vmem] * 5,
        out_specs=(hbm,) * 2,
        scratch_shapes=[pltpu.VMEM((ROWS, WIDTH), BF16), pltpu.SemaphoreType.DMA((2,))],
        compiler_params=pltpu.CompilerParams(vmem_limit_bytes=12 << 20),
        name="finish",
    )(total, means, w2n_rows, fresh, gain_two.reshape(1, WIDTH))


def solution(mesh):
    nodes = P(("blk", "narrow"), None)
    return jax.shard_map(
        body,
        mesh=mesh,
        in_specs=(nodes, nodes, nodes, P(("blk", "narrow")), P(("blk", "narrow"), None, None, None)) + (P(),) * 8,
        out_specs=(nodes, nodes),
        check_vma=False,
    )
```
